256 devices in a mesh: dp: 32 (over y, z_hi, core), expert: 8 (over z_lo, x).
Axes of the slice: x: 4, y: 4, z: 8 (z_hi: 4, z_lo: 2; z = z_hi * 2 + z_lo), core: 2. Of those that a mesh axis runs over, the one named last changes fastest.
Arguments:
- gradients: bfloat16 [512, 1024, 768], P('expert', 'dp'), may hold values from -32 to 32
- momentum: bfloat16 [512, 1024, 768], P('expert', 'dp'), may hold values from -6 to 6
Outputs:
- update: bfloat16 [512, 1024, 768], P('expert', 'dp')
- new_momentum: bfloat16 [512, 1024, 768], P('expert', 'dp')
The draws below stay inside these ranges and needn't reach their ends.
All inputs are finite; a program needn't handle non-finite values.
Results may differ from the reference program's by a relative error of at most 0.0071.
Values may be sent and summed in bfloat16 or wider, within the bound.
No kernel may reach another device: no remote copies, remote signals or barrier semaphores. Data moves between devices by JAX's collectives and lax.ppermute only.
A program may use at most 64 MiB of HBM per device.

```python
import math
import jax
import jax.numpy as jnp
from jax import lax

D = 1024
FE = 768
ITERS = 2
TOTAL = 512


def draw_gradients(key, part):
    key = jax.random.fold_in(key, 7)
    row_key, col_key, main_key = jax.random.split(key, 3)
    position = jnp.arange(TOTAL, dtype=jnp.float32)[:, None, None] / (TOTAL - 1)
    row_scale = jnp.exp(jax.random.uniform(row_key, (1, D, 1), jnp.float32, 0.0, math.log(10.0)))
    col_scale = jnp.exp(jax.random.uniform(col_key, (1, 1, FE), jnp.float32, 0.0, math.log(10.0)))
    sample = jax.random.truncated_normal(main_key, -4.0, 4.0, (TOTAL, D, FE), jnp.float32)
    values = sample * row_scale * col_scale * (1.0 + 2.0 * position) * 0.05
    return jnp.clip(values, -32.0, 32.0).astype(jnp.bfloat16)


def levels(rng, shape, cuts, smallest, largest):
    def one(axis_at, blocks):
        steps = jax.random.uniform(jax.random.fold_in(jax.random.fold_in(rng, 6), axis_at), (blocks,), jnp.float32, smallest / len(cuts), largest / len(cuts))
        return jnp.repeat(jnp.exp(steps), shape[axis_at] // blocks).reshape((-1,) + (1,) * (len(shape) - axis_at - 1))

    level = one(*cuts[0])
    for cut in cuts[1:]:
        level = level * one(*cut)
    return level


def gaussian(rng, extent, deviation, most, pieces=(), kind=jnp.bfloat16):
    values = deviation * jax.random.normal(rng, extent, jnp.float32)
    if pieces:
        values = values * levels(rng, extent, pieces, -0.22, 0.18)
    return jnp.clip(values, -most, most).astype(kind)


def setup_inputs(seed: int = 0) -> dict:
    key_list = jax.random.split(jax.random.key(seed), 3)
    gradients = draw_gradients(jax.random.fold_in(key_list[2], 71), 0)
    momentum = gaussian(key_list[1], (TOTAL, D, FE), 0.5, 6.0, ((0, 8), (1, 32)))
    return dict(gradients=gradients, momentum=momentum)


MU = 0.95
COEF_A = 3.4445
COEF_B = -4.775
COEF_C = 2.0315
CLIP_RMS = 0.25

def orthogonal_update(new_moment):
    values = lax.optimization_barrier(new_moment).astype(jnp.float32)
    orthogonal = (values / (jnp.sqrt(jnp.sum(values * values)) + 1e-07)).astype(jnp.bfloat16)
    for iteration in range(ITERS):
        orthogonal = lax.optimization_barrier(orthogonal)
        gram_matrix = jnp.dot(orthogonal.T, orthogonal, preferred_element_type=jnp.float32).astype(jnp.bfloat16)
        gram_matrix = lax.optimization_barrier(gram_matrix)
        squared = jnp.dot(gram_matrix, gram_matrix, preferred_element_type=jnp.float32)
        polynomial = (COEF_B * gram_matrix.astype(jnp.float32) + COEF_C * squared).astype(jnp.bfloat16)
        orthogonal = (COEF_A * orthogonal.astype(jnp.float32) + jnp.dot(orthogonal, polynomial, preferred_element_type=jnp.float32)).astype(jnp.bfloat16)
    orthogonal = lax.optimization_barrier(orthogonal)
    rms_scale = 0.2 * math.sqrt(max(D, FE))
    return (rms_scale * orthogonal.astype(jnp.float32)).astype(jnp.bfloat16)

def reference(gradients, momentum):
    entries = gradients.shape[0] * D * FE

    def squares(matrix):
        values = matrix.astype(jnp.float32)
        return jnp.sum(values * values)
    total_squares = jnp.sum(lax.map(squares, gradients))
    factor = CLIP_RMS * math.sqrt(entries) / (jnp.sqrt(total_squares) + 1e-06)

    def one_matrix(pair):
        buffer = MU * pair[1].astype(jnp.float32) + factor * pair[0].astype(jnp.float32)
        fresh = buffer.astype(jnp.bfloat16)
        return (orthogonal_update(fresh), fresh)
    update, new_momentum = lax.map(one_matrix, (gradients, momentum))
    return (update, new_momentum)
```

```python
import functools
import math

import jax
import jax.numpy as jnp
from jax import lax
from jax.experimental import pallas as pl
from jax.experimental.pallas import tpu as pltpu
from jax.sharding import PartitionSpec as P

ITERS = 2

MU = 0.95
COEF_A = 3.4445
COEF_B = -4.775
COEF_C = 2.0315
CLIP_RMS = 0.25
VMEM_LIMIT = 56 * 1024 * 1024
BLOCK = 8


def square_kernel(g_ref, o_ref):
    @pl.when(pl.program_id(0) == 0)
    def _():
        o_ref[...] = jnp.zeros_like(o_ref)

    values = g_ref[...].astype(jnp.float32)
    squares = values * values
    o_ref[...] += jnp.sum(squares.reshape(-1, 8, squares.shape[-1]), axis=0)


def local_squares(gradients):
    count, rows, width = gradients.shape
    partial = pl.pallas_call(
        square_kernel,
        grid=(count // BLOCK,),
        in_specs=[pl.BlockSpec((BLOCK, rows, width), lambda i: (i, 0, 0))],
        out_specs=pl.BlockSpec((8, width), lambda i: (0, 0)),
        out_shape=jax.ShapeDtypeStruct((8, width), jnp.float32),
    )(gradients)
    return jnp.sum(partial)


def all_sum(value, axis):
    size = lax.axis_size(axis)
    copies = jnp.broadcast_to(value, (size, 8, 128))
    return jnp.sum(lax.all_to_all(copies, axis, 0, 0)[:, 0, 0])


def fresh_kernel(f_ref, g_ref, m_ref, *refs):
    buffer = MU * m_ref[...].astype(jnp.float32) + f_ref[0] * g_ref[...].astype(jnp.float32)
    fresh = buffer.astype(jnp.bfloat16)
    for ref in refs[-2:]:
        ref[...] = fresh


def fresh_half(factor, gradients, momentum, half, kept):
    count, rows, width = gradients.shape
    steps = count // 2 // BLOCK
    block = (BLOCK, rows, width)
    here = pl.BlockSpec(block, lambda i: (half * steps + i, 0, 0))
    in_specs = [pl.BlockSpec(memory_space=pltpu.SMEM), here, here]
    args = [factor.reshape(1), gradients, momentum]
    aliases = {}
    if kept is not None:
        in_specs.append(pl.BlockSpec(memory_space=pl.ANY))
        args.append(kept)
        aliases = {3: 0}
    return pl.pallas_call(
        fresh_kernel,
        grid=(steps,),
        in_specs=in_specs,
        out_specs=[here, pl.BlockSpec(block, lambda i: (i, 0, 0))],
        out_shape=[
            jax.ShapeDtypeStruct(gradients.shape, jnp.bfloat16),
            jax.ShapeDtypeStruct((count // 2, rows, width), jnp.bfloat16),
        ],
        input_output_aliases=aliases,
    )(*args)


def place_kernel(part_ref, *refs):
    refs[-1][...] = part_ref[...]


def place_half(part, half, whole):
    count, rows, width = part.shape
    steps = count // BLOCK
    block = (BLOCK, rows, width)
    in_specs = [pl.BlockSpec(block, lambda i: (i, 0, 0))]
    args = [part]
    aliases = {}
    if whole is not None:
        in_specs.append(pl.BlockSpec(memory_space=pl.ANY))
        args.append(whole)
        aliases = {1: 0}
    return pl.pallas_call(
        place_kernel,
        grid=(steps,),
        in_specs=in_specs,
        out_specs=pl.BlockSpec(block, lambda i: (half * steps + i, 0, 0)),
        out_shape=jax.ShapeDtypeStruct((2 * count, rows, width), jnp.bfloat16),
        input_output_aliases=aliases,
    )(*args)


def ortho_kernel(x_ref, out_ref, ortho, gram, poly):
    rows, width = x_ref.shape
    tile = 256
    scale = 0.2 * math.sqrt(max(rows, width))

    def square_tile(i, total):
        values = x_ref[pl.ds(pl.multiple_of(i * tile, tile), tile), :].astype(jnp.float32)
        return total + jnp.sum((values * values).reshape(-1, 8, width), axis=0)

    total = lax.fori_loop(0, rows // tile, square_tile, jnp.zeros((8, width), jnp.float32))
    inverse = 1.0 / (jnp.sqrt(jnp.sum(total)) + 1e-07)

    def normalize(i, carry):
        here = pl.ds(pl.multiple_of(i * tile, tile), tile)
        ortho[here, :] = (x_ref[here, :].astype(jnp.float32) * inverse).astype(jnp.bfloat16)
        return carry

    lax.fori_loop(0, rows // tile, normalize, 0)

    for iteration in range(ITERS):
        for i in range(width // tile):
            here = slice(i * tile, (i + 1) * tile)
            gram[here, :] = lax.dot_general(
                ortho[:, here], ortho[...], (((0,), (0,)), ((), ())),
                preferred_element_type=jnp.float32,
            ).astype(jnp.bfloat16)
        for i in range(width // tile):
            here = slice(i * tile, (i + 1) * tile)
            squared = jnp.dot(gram[here, :], gram[...], preferred_element_type=jnp.float32)
            poly[here, :] = (
                COEF_B * gram[here, :].astype(jnp.float32) + COEF_C * squared
            ).astype(jnp.bfloat16)
        for i in range(rows // tile):
            here = slice(i * tile, (i + 1) * tile)
            product = jnp.dot(ortho[here, :], poly[...], preferred_element_type=jnp.float32)
            result = (COEF_A * ortho[here, :].astype(jnp.float32) + product).astype(jnp.bfloat16)
            if iteration == ITERS - 1:
                out_ref[here, :] = (scale * result.astype(jnp.float32)).astype(jnp.bfloat16)
            else:
                ortho[here, :] = result


def orthogonal_update(matrix):
    rows, width = matrix.shape
    flops = ITERS * (4 * rows * width * width + 2 * width**3)
    return pl.pallas_call(
        ortho_kernel,
        in_specs=[pl.BlockSpec(memory_space=pltpu.VMEM)],
        out_specs=pl.BlockSpec(memory_space=pltpu.VMEM),
        out_shape=jax.ShapeDtypeStruct(matrix.shape, jnp.bfloat16),
        scratch_shapes=[
            pltpu.VMEM((rows, width), jnp.bfloat16),
            pltpu.VMEM((width, width), jnp.bfloat16),
            pltpu.VMEM((width, width), jnp.bfloat16),
        ],
        compiler_params=pltpu.CompilerParams(vmem_limit_bytes=VMEM_LIMIT),
        cost_estimate=pl.CostEstimate(
            flops=flops, bytes_accessed=4 * rows * width, transcendentals=0
        ),
    )(matrix)


def shards(gradients, momentum):
    dp_count = lax.axis_size("dp")
    unit_count, shard_rows, width = gradients.shape
    rows = shard_rows * dp_count
    entries = unit_count * lax.axis_size("expert") * rows * width
    total_squares = all_sum(all_sum(local_squares(gradients), "dp"), "expert")
    factor = CLIP_RMS * math.sqrt(entries) / (jnp.sqrt(total_squares) + 1e-06)

    kept, send0 = fresh_half(factor, gradients, momentum, 0, None)
    owned0 = lax.all_to_all(send0, "dp", 0, 0)
    kept, send1 = fresh_half(factor, gradients, momentum, 1, kept)
    owned1 = lax.all_to_all(send1, "dp", 0, 0)
    update0 = orthogonal_update(owned0.reshape(rows, width))
    home0 = lax.all_to_all(update0.reshape(dp_count, shard_rows, width), "dp", 0, 0)
    update1 = orthogonal_update(owned1.reshape(rows, width))
    home1 = lax.all_to_all(update1.reshape(dp_count, shard_rows, width), "dp", 0, 0)
    whole = place_half(home0, 0, None)
    whole = place_half(home1, 1, whole)
    return whole, kept


def solution(mesh):
    in_specs = (P("expert", "dp", None), P("expert", "dp", None))
    out_specs = (P("expert", "dp", None), P("expert", "dp", None))
    return jax.shard_map(shards, mesh=mesh, in_specs=in_specs, out_specs=out_specs, check_vma=False)
```

```python
import math

import jax
import jax.numpy as jnp
from jax import lax
from jax.experimental import pallas as pl
from jax.experimental.pallas import tpu as pltpu
from jax.sharding import PartitionSpec as P

ITERS = 2

MU = 0.95
COEF_A = 3.4445
COEF_B = -4.775
COEF_C = 2.0315
CLIP_RMS = 0.25
TILE = 256
SMALL = pltpu.CompilerParams(vmem_limit_bytes=16 * 1024 * 1024)
LARGE = pltpu.CompilerParams(vmem_limit_bytes=28 * 1024 * 1024)
VMEM = pl.BlockSpec(memory_space=pltpu.VMEM)


def square_kernel(g_ref, o_ref):
    count, rows, width = g_ref.shape

    def add(i, total):
        values = g_ref[pl.ds(i * 2, 2)].astype(jnp.float32)
        return total + jnp.sum((values * values).reshape(-1, 8, width), axis=0)

    total = lax.fori_loop(0, count // 2, add, jnp.zeros((8, width), jnp.float32), unroll=4)
    o_ref[...] = jnp.full(o_ref.shape, jnp.sum(total), jnp.float32)


def copies_of_squares(gradients, copies):
    return pl.pallas_call(
        square_kernel,
        in_specs=[VMEM],
        out_specs=VMEM,
        out_shape=jax.ShapeDtypeStruct((copies, 8, 128), jnp.float32),
        compiler_params=SMALL,
    )(gradients)


def sum_kernel(i_ref, o_ref):
    o_ref[...] = jnp.broadcast_to(jnp.sum(i_ref[...], axis=0, keepdims=True), o_ref.shape)


def copies_of_sum(parts, copies):
    return pl.pallas_call(
        sum_kernel,
        in_specs=[VMEM],
        out_specs=VMEM,
        out_shape=jax.ShapeDtypeStruct((copies, 8, 128), jnp.float32),
        compiler_params=SMALL,
    )(parts)


def fresh_momentum(parts, gradients, momentum, entries):
    def kernel(p_ref, g_ref, m_ref, o_ref):
        total = jnp.sum(p_ref[...], axis=0, keepdims=True)[:, :1, :1]
        factor = CLIP_RMS * math.sqrt(entries) / (jnp.sqrt(total) + 1e-06)

        def step(i, carry):
            here = pl.ds(i * 2, 2)
            buffer = MU * m_ref[here].astype(jnp.float32) + factor * g_ref[here].astype(jnp.float32)
            o_ref[here] = buffer.astype(jnp.bfloat16)
            return carry

        lax.fori_loop(0, g_ref.shape[0] // 2, step, 0, unroll=2)

    return pl.pallas_call(
        kernel,
        in_specs=[VMEM] * 3,
        out_specs=VMEM,
        out_shape=jax.ShapeDtypeStruct(gradients.shape, jnp.bfloat16),
        compiler_params=SMALL,
    )(parts, gradients, momentum)


def keep_kernel(i_ref, *refs):
    refs[-1][...] = i_ref[...]


def keep_half(source, half, kept):
    count, rows, width = source.shape
    block = count // 8
    here = pl.BlockSpec((block, rows, width), lambda i: (half * 4 + i, 0, 0))
    in_specs, args, aliases = [here], [source], {}
    if kept is not None:
        in_specs.append(pl.BlockSpec(memory_space=pl.ANY))
        args.append(kept)
        aliases = {1: 0}
    return pl.pallas_call(
        keep_kernel,
        grid=(4,),
        in_specs=in_specs,
        out_specs=here,
        out_shape=jax.ShapeDtypeStruct(source.shape, jnp.bfloat16),
        input_output_aliases=aliases,
        compiler_params=SMALL,
    )(*args)


def ortho_kernel(x_ref, out_ref, ortho, gram, poly):
    source, out = x_ref.at[:, 0], out_ref.at[:, 0]
    pieces, piece, width = source.shape
    rows = pieces * piece
    step = TILE // piece
    scale = 0.2 * math.sqrt(max(rows, width))

    total = jnp.zeros((8, width), jnp.float32)
    for i in range(rows // TILE):
        values = source[i * step:(i + 1) * step].astype(jnp.float32)
        total += jnp.sum((values * values).reshape(-1, 8, width), axis=0)
    inverse = 1.0 / (jnp.sqrt(jnp.sum(total)) + 1e-07)
    for i in range(rows // TILE):
        values = source[i * step:(i + 1) * step].astype(jnp.float32).reshape(TILE, width)
        ortho[i * TILE:(i + 1) * TILE, :] = (values * inverse).astype(jnp.bfloat16)

    for iteration in range(ITERS):
        for i in range(width // TILE):
            here, right = slice(i * TILE, (i + 1) * TILE), slice(i * TILE, width)
            tiles = lax.dot_general(
                ortho[:, here], ortho[:, right], (((0,), (0,)), ((), ())),
                preferred_element_type=jnp.float32,
            ).astype(jnp.bfloat16)
            gram[here, right] = tiles
            for j in range(i + 1, width // TILE):
                gram[j * TILE:(j + 1) * TILE, here] = tiles[:, (j - i) * TILE:(j - i + 1) * TILE].T
        for i in range(width // TILE):
            here, right = slice(i * TILE, (i + 1) * TILE), slice(i * TILE, width)
            squared = jnp.dot(gram[here, :], gram[:, right], preferred_element_type=jnp.float32)
            tiles = (COEF_B * gram[here, right].astype(jnp.float32) + COEF_C * squared).astype(
                jnp.bfloat16
            )
            poly[here, right] = tiles
            for j in range(i + 1, width // TILE):
                poly[j * TILE:(j + 1) * TILE, here] = tiles[:, (j - i) * TILE:(j - i + 1) * TILE].T
        for i in range(rows // TILE):
            here = slice(i * TILE, (i + 1) * TILE)
            product = jnp.dot(ortho[here, :], poly[...], preferred_element_type=jnp.float32)
            result = (COEF_A * ortho[here, :].astype(jnp.float32) + product).astype(jnp.bfloat16)
            if iteration == ITERS - 1:
                update = (scale * result.astype(jnp.float32)).astype(jnp.bfloat16)
                out[i * step:(i + 1) * step] = update.reshape(step, piece, width)
            else:
                ortho[here, :] = result


def orthogonal_updates(matrices):
    pieces, count, piece, width = matrices.shape
    rows = pieces * piece
    here = pl.BlockSpec((pieces, 1, piece, width), lambda i: (0, i, 0, 0))
    return pl.pallas_call(
        ortho_kernel,
        grid=(count,),
        in_specs=[here],
        out_specs=here,
        out_shape=jax.ShapeDtypeStruct(matrices.shape, jnp.bfloat16),
        scratch_shapes=[
            pltpu.VMEM((rows, width), jnp.bfloat16),
            pltpu.VMEM((width, width), jnp.bfloat16),
            pltpu.VMEM((width, width), jnp.bfloat16),
        ],
        compiler_params=LARGE,
        cost_estimate=pl.CostEstimate(
            flops=count * ITERS * (4 * rows * width * width + 2 * width**3),
            bytes_accessed=4 * count * rows * width,
            transcendentals=0,
        ),
    )(matrices)


def shards(gradients, momentum):
    dp_count, expert_count = lax.axis_size("dp"), lax.axis_size("expert")
    unit_count, shard_rows, width = gradients.shape
    split = (dp_count, unit_count // dp_count, shard_rows, width)
    entries = unit_count * expert_count * shard_rows * dp_count * width

    parts = lax.all_to_all(copies_of_squares(gradients, dp_count), "dp", 0, 0)
    parts = lax.all_to_all(copies_of_sum(parts, expert_count), "expert", 0, 0)
    fresh = fresh_momentum(parts, gradients, momentum, entries)

    owned = lax.all_to_all(fresh.reshape(split), "dp", 0, 0)
    kept = keep_half(fresh, 0, None)
    updates = orthogonal_updates(owned)
    home = lax.all_to_all(updates, "dp", 0, 0)
    fresh, updates = lax.optimization_barrier((fresh, updates))
    kept = keep_half(fresh, 1, kept)
    return home.reshape(unit_count, shard_rows, width), kept


def solution(mesh):
    in_specs = (P("expert", "dp", None), P("expert", "dp", None))
    out_specs = (P("expert", "dp", None), P("expert", "dp", None))
    return jax.shard_map(shards, mesh=mesh, in_specs=in_specs, out_specs=out_specs, check_vma=False)
```

```python
import math

import jax
import jax.numpy as jnp
from jax import lax
from jax.experimental import pallas as pl
from jax.experimental.pallas import tpu as pltpu
from jax.sharding import PartitionSpec as P

ITERS = 2

MU = 0.95
COEF_A = 3.4445
COEF_B = -4.775
COEF_C = 2.0315
CLIP_RMS = 0.25
TILE = 256
SMALL = pltpu.CompilerParams(vmem_limit_bytes=16 * 1024 * 1024)
LARGE = pltpu.CompilerParams(vmem_limit_bytes=28 * 1024 * 1024)
VMEM = pl.BlockSpec(memory_space=pltpu.VMEM)
HBM = pl.BlockSpec(memory_space=pltpu.HBM)
CHUNKS = 4
ORDER = [[y * 8 + z * 2 + core for y in range(4) for core in range(2) for z in range(4)]]


def square_kernel(g_ref, o_ref):
    count, rows, width = g_ref.shape

    def add(i, total):
        values = g_ref[pl.ds(i * 2, 2)].astype(jnp.float32)
        return total + jnp.sum((values * values).reshape(-1, 8, width), axis=0)

    total = lax.fori_loop(0, count // 2, add, jnp.zeros((8, width), jnp.float32), unroll=4)
    o_ref[...] = jnp.full(o_ref.shape, jnp.sum(total), jnp.float32)


def copies_of_squares(gradients, copies):
    return pl.pallas_call(
        square_kernel,
        in_specs=[VMEM],
        out_specs=VMEM,
        out_shape=jax.ShapeDtypeStruct((copies, 8, 128), jnp.float32),
        compiler_params=SMALL,
    )(gradients)


def sum_kernel(i_ref, o_ref):
    o_ref[...] = jnp.broadcast_to(jnp.sum(i_ref[...], axis=0, keepdims=True), o_ref.shape)


def copies_of_sum(parts, copies):
    return pl.pallas_call(
        sum_kernel,
        in_specs=[VMEM],
        out_specs=VMEM,
        out_shape=jax.ShapeDtypeStruct((copies, 8, 128), jnp.float32),
        compiler_params=SMALL,
    )(parts)


def fresh_momentum(parts, gradients, momentum, entries):
    count, rows, width = gradients.shape
    chunk = count // CHUNKS

    def kernel(p_ref, g_ref, m_ref, o_ref, k_ref, m_vmem, m_sems, k_sems):
        def part(i):
            return pl.ds(i * chunk, chunk)

        loads = [
            pltpu.make_async_copy(m_ref.at[part(i)], m_vmem.at[part(i)], m_sems.at[i])
            for i in range(CHUNKS)
        ]
        stores = [
            pltpu.make_async_copy(o_ref.at[part(i)], k_ref.at[part(i)], k_sems.at[i])
            for i in range(CHUNKS)
        ]
        for load in loads:
            load.start()
        total = jnp.sum(p_ref[...], axis=0, keepdims=True)[:, :1, :1]
        factor = CLIP_RMS * math.sqrt(entries) / (jnp.sqrt(total) + 1e-06)

        def step(i, carry):
            here = pl.ds(i * 2, 2)
            buffer = MU * m_vmem[here].astype(jnp.float32) + factor * g_ref[here].astype(jnp.float32)
            o_ref[here] = buffer.astype(jnp.bfloat16)
            return carry

        for i in range(CHUNKS):
            loads[i].wait()
            lax.fori_loop(i * chunk // 2, (i + 1) * chunk // 2, step, 0, unroll=2)
            stores[i].start()
        for store in stores:
            store.wait()

    return pl.pallas_call(
        kernel,
        in_specs=[VMEM, VMEM, HBM],
        out_specs=[VMEM, HBM],
        out_shape=[jax.ShapeDtypeStruct(gradients.shape, jnp.bfloat16)] * 2,
        scratch_shapes=[
            pltpu.VMEM(gradients.shape, jnp.bfloat16),
            pltpu.SemaphoreType.DMA((CHUNKS,)),
            pltpu.SemaphoreType.DMA((CHUNKS,)),
        ],
        compiler_params=SMALL,
    )(parts, gradients, momentum)


def ortho_kernel(x_ref, out_ref, ortho, gram, poly):
    for i in range(x_ref.shape[1]):
        newton_schulz(x_ref.at[:, i], out_ref.at[:, i], ortho, gram, poly)


def newton_schulz(source, out, ortho, gram, poly):
    pieces, piece, width = source.shape
    rows = pieces * piece
    step = TILE // piece
    scale = 0.2 * math.sqrt(max(rows, width))

    total = jnp.zeros((8, width), jnp.float32)
    for i in range(rows // TILE):
        values = source[i * step:(i + 1) * step].astype(jnp.float32)
        total += jnp.sum((values * values).reshape(-1, 8, width), axis=0)
    inverse = 1.0 / (jnp.sqrt(jnp.sum(total)) + 1e-07)
    for i in range(rows // TILE):
        values = source[i * step:(i + 1) * step].astype(jnp.float32).reshape(TILE, width)
        ortho[i * TILE:(i + 1) * TILE, :] = (values * inverse).astype(jnp.bfloat16)

    for iteration in range(ITERS):
        for i in range(width // TILE):
            here, right = slice(i * TILE, (i + 1) * TILE), slice(i * TILE, width)
            tiles = lax.dot_general(
                ortho[:, here], ortho[:, right], (((0,), (0,)), ((), ())),
                preferred_element_type=jnp.float32,
            ).astype(jnp.bfloat16)
            gram[here, right] = tiles
            for j in range(i + 1, width // TILE):
                gram[j * TILE:(j + 1) * TILE, here] = tiles[:, (j - i) * TILE:(j - i + 1) * TILE].T
        for i in range(width // TILE):
            here, right = slice(i * TILE, (i + 1) * TILE), slice(i * TILE, width)
            squared = jnp.dot(gram[here, :], gram[:, right], preferred_element_type=jnp.float32)
            tiles = (COEF_B * gram[here, right].astype(jnp.float32) + COEF_C * squared).astype(
                jnp.bfloat16
            )
            poly[here, right] = tiles
            for j in range(i + 1, width // TILE):
                poly[j * TILE:(j + 1) * TILE, here] = tiles[:, (j - i) * TILE:(j - i + 1) * TILE].T
        for i in range(rows // TILE):
            here = slice(i * TILE, (i + 1) * TILE)
            product = jnp.dot(ortho[here, :], poly[...], preferred_element_type=jnp.float32)
            result = (COEF_A * ortho[here, :].astype(jnp.float32) + product).astype(jnp.bfloat16)
            if iteration == ITERS - 1:
                update = (scale * result.astype(jnp.float32)).astype(jnp.bfloat16)
                out[i * step:(i + 1) * step] = update.reshape(step, piece, width)
            else:
                ortho[here, :] = result


def orthogonal_updates(matrices):
    pieces, count, piece, width = matrices.shape
    rows = pieces * piece
    return pl.pallas_call(
        ortho_kernel,
        in_specs=[VMEM],
        out_specs=VMEM,
        out_shape=jax.ShapeDtypeStruct(matrices.shape, jnp.bfloat16),
        scratch_shapes=[
            pltpu.VMEM((rows, width), jnp.bfloat16),
            pltpu.VMEM((width, width), jnp.bfloat16),
            pltpu.VMEM((width, width), jnp.bfloat16),
        ],
        compiler_params=LARGE,
        cost_estimate=pl.CostEstimate(
            flops=count * ITERS * (4 * rows * width * width + 2 * width**3),
            bytes_accessed=4 * count * rows * width,
            transcendentals=0,
        ),
    )(matrices)


def shards(gradients, momentum):
    dp_count, expert_count = lax.axis_size("dp"), lax.axis_size("expert")
    unit_count, shard_rows, width = gradients.shape
    split = (dp_count, unit_count // dp_count, shard_rows, width)
    entries = unit_count * expert_count * shard_rows * dp_count * width

    parts = lax.all_to_all(copies_of_squares(gradients, dp_count), "dp", 0, 0)
    parts = lax.all_to_all(copies_of_sum(parts, expert_count), "expert", 0, 0)
    fresh, kept = fresh_momentum(parts, gradients, momentum, entries)

    owned = lax.all_to_all(fresh.reshape(split), "dp", 0, 0, axis_index_groups=ORDER)
    home = lax.all_to_all(orthogonal_updates(owned), "dp", 0, 0, axis_index_groups=ORDER)
    return home.reshape(unit_count, shard_rows, width), kept


def solution(mesh):
    in_specs = (P("expert", "dp", None), P("expert", "dp", None))
    out_specs = (P("expert", "dp", None), P("expert", "dp", None))
    return jax.shard_map(shards, mesh=mesh, in_specs=in_specs, out_specs=out_specs, check_vma=False)
```

```python
import math

import jax
import jax.numpy as jnp
from jax import lax
from jax.experimental import pallas as pl
from jax.experimental.pallas import tpu as pltpu
from jax.sharding import PartitionSpec as P

ITERS = 2

MU = 0.95
COEF_A = 3.4445
COEF_B = -4.775
COEF_C = 2.0315
CLIP_RMS = 0.25
TILE = 256
SMALL = pltpu.CompilerParams(vmem_limit_bytes=16 * 1024 * 1024)
LARGE = pltpu.CompilerParams(vmem_limit_bytes=28 * 1024 * 1024)
VMEM = pl.BlockSpec(memory_space=pltpu.VMEM)
HBM = pl.BlockSpec(memory_space=pltpu.HBM)
CHUNKS = 4
ORDER = [[y * 8 + z * 2 + core for y in range(4) for core in range(2) for z in range(4)]]
AXES = ("dp", "expert")


def device(x, y, z, core):
    return (y * 8 + z // 2 * 2 + core) * 8 + z % 2 * 4 + x


COLUMNS = [
    [device(x, y, z, core) for z in range(8) for core in range(2)]
    for x in range(4) for y in range(4)
]
PLANES = [
    [device(x, y, z, core) for y in range(4) for x in range(4)]
    for z in range(8) for core in range(2)
]


def square_kernel(g_ref, o_ref):
    count, rows, width = g_ref.shape

    def add(i, total):
        values = g_ref[pl.ds(i * 2, 2)].astype(jnp.float32)
        return total + jnp.sum((values * values).reshape(-1, 8, width), axis=0)

    total = lax.fori_loop(0, count // 2, add, jnp.zeros((8, width), jnp.float32), unroll=4)
    o_ref[...] = jnp.full(o_ref.shape, jnp.sum(total), jnp.float32)


def copies_of_squares(gradients, copies):
    return pl.pallas_call(
        square_kernel,
        in_specs=[VMEM],
        out_specs=VMEM,
        out_shape=jax.ShapeDtypeStruct((copies, 1, 128), jnp.float32),
        compiler_params=SMALL,
    )(gradients)


def sum_kernel(i_ref, o_ref):
    o_ref[...] = jnp.broadcast_to(jnp.sum(i_ref[...], axis=0, keepdims=True), o_ref.shape)


def copies_of_sum(parts, copies):
    return pl.pallas_call(
        sum_kernel,
        in_specs=[VMEM],
        out_specs=VMEM,
        out_shape=jax.ShapeDtypeStruct((copies, 1, 128), jnp.float32),
        compiler_params=SMALL,
    )(parts)


def fresh_momentum(parts, gradients, momentum, entries):
    count, rows, width = gradients.shape
    chunk = count // CHUNKS

    def kernel(p_ref, g_ref, m_ref, o_ref, k_ref, m_vmem, m_sems, k_sems):
        def part(i):
            return pl.ds(i * chunk, chunk)

        loads = [
            pltpu.make_async_copy(m_ref.at[part(i)], m_vmem.at[part(i)], m_sems.at[i])
            for i in range(CHUNKS)
        ]
        stores = [
            pltpu.make_async_copy(o_ref.at[part(i)], k_ref.at[part(i)], k_sems.at[i])
            for i in range(CHUNKS)
        ]
        for load in loads:
            load.start()
        total = jnp.sum(p_ref[...], axis=0, keepdims=True)[:, :1, :1]
        factor = CLIP_RMS * math.sqrt(entries) / (jnp.sqrt(total) + 1e-06)

        def step(i, carry):
            here = pl.ds(i * 2, 2)
            buffer = MU * m_vmem[here].astype(jnp.float32) + factor * g_ref[here].astype(jnp.float32)
            o_ref[here] = buffer.astype(jnp.bfloat16)
            return carry

        for i in range(CHUNKS):
            loads[i].wait()
            lax.fori_loop(i * chunk // 2, (i + 1) * chunk // 2, step, 0, unroll=2)
            stores[i].start()
        for store in stores:
            store.wait()

    return pl.pallas_call(
        kernel,
        in_specs=[VMEM, VMEM, HBM],
        out_specs=[VMEM, HBM],
        out_shape=[jax.ShapeDtypeStruct(gradients.shape, jnp.bfloat16)] * 2,
        scratch_shapes=[
            pltpu.VMEM(gradients.shape, jnp.bfloat16),
            pltpu.SemaphoreType.DMA((CHUNKS,)),
            pltpu.SemaphoreType.DMA((CHUNKS,)),
        ],
        compiler_params=SMALL,
    )(parts, gradients, momentum)


def ortho_kernel(x_ref, out_ref, ortho, gram, poly):
    for i in range(x_ref.shape[1]):
        newton_schulz(x_ref.at[:, i], out_ref.at[:, i], ortho, gram, poly)


def newton_schulz(source, out, ortho, gram, poly):
    pieces, piece, width = source.shape
    rows = pieces * piece
    step = TILE // piece
    scale = 0.2 * math.sqrt(max(rows, width))

    total = jnp.zeros((8, width), jnp.float32)
    for i in range(rows // TILE):
        values = source[i * step:(i + 1) * step].astype(jnp.float32)
        total += jnp.sum((values * values).reshape(-1, 8, width), axis=0)
    inverse = 1.0 / (jnp.sqrt(jnp.sum(total)) + 1e-07)
    for i in range(rows // TILE):
        values = source[i * step:(i + 1) * step].astype(jnp.float32).reshape(TILE, width)
        ortho[i * TILE:(i + 1) * TILE, :] = (values * inverse).astype(jnp.bfloat16)

    for iteration in range(ITERS):
        for i in range(width // TILE):
            here, right = slice(i * TILE, (i + 1) * TILE), slice(i * TILE, width)
            tiles = lax.dot_general(
                ortho[:, here], ortho[:, right], (((0,), (0,)), ((), ())),
                preferred_element_type=jnp.float32,
            ).astype(jnp.bfloat16)
            gram[here, right] = tiles
            for j in range(i + 1, width // TILE):
                gram[j * TILE:(j + 1) * TILE, here] = tiles[:, (j - i) * TILE:(j - i + 1) * TILE].T
        for i in range(width // TILE):
            here, right = slice(i * TILE, (i + 1) * TILE), slice(i * TILE, width)
            squared = jnp.dot(gram[here, :], gram[:, right], preferred_element_type=jnp.float32)
            tiles = (COEF_B * gram[here, right].astype(jnp.float32) + COEF_C * squared).astype(
                jnp.bfloat16
            )
            poly[here, right] = tiles
            for j in range(i + 1, width // TILE):
                poly[j * TILE:(j + 1) * TILE, here] = tiles[:, (j - i) * TILE:(j - i + 1) * TILE].T
        for i in range(rows // TILE):
            here = slice(i * TILE, (i + 1) * TILE)
            product = jnp.dot(ortho[here, :], poly[...], preferred_element_type=jnp.float32)
            result = (COEF_A * ortho[here, :].astype(jnp.float32) + product).astype(jnp.bfloat16)
            if iteration == ITERS - 1:
                update = (scale * result.astype(jnp.float32)).astype(jnp.bfloat16)
                out[i * step:(i + 1) * step] = update.reshape(step, piece, width)
            else:
                ortho[here, :] = result


def orthogonal_updates(matrices):
    pieces, count, piece, width = matrices.shape
    rows = pieces * piece
    return pl.pallas_call(
        ortho_kernel,
        in_specs=[VMEM],
        out_specs=VMEM,
        out_shape=jax.ShapeDtypeStruct(matrices.shape, jnp.bfloat16),
        scratch_shapes=[
            pltpu.VMEM((rows, width), jnp.bfloat16),
            pltpu.VMEM((width, width), jnp.bfloat16),
            pltpu.VMEM((width, width), jnp.bfloat16),
        ],
        compiler_params=LARGE,
        cost_estimate=pl.CostEstimate(
            flops=count * ITERS * (4 * rows * width * width + 2 * width**3),
            bytes_accessed=4 * count * rows * width,
            transcendentals=0,
        ),
    )(matrices)


def shards(gradients, momentum):
    dp_count, expert_count = lax.axis_size("dp"), lax.axis_size("expert")
    unit_count, shard_rows, width = gradients.shape
    split = (dp_count, unit_count // dp_count, shard_rows, width)
    entries = unit_count * expert_count * shard_rows * dp_count * width

    parts = copies_of_squares(gradients, len(COLUMNS[0]))
    parts = lax.all_to_all(parts, AXES, 0, 0, axis_index_groups=COLUMNS)
    parts = copies_of_sum(parts, len(PLANES[0]))
    parts = lax.all_to_all(parts, AXES, 0, 0, axis_index_groups=PLANES)
    fresh, kept = fresh_momentum(parts, gradients, momentum, entries)

    owned = lax.all_to_all(fresh.reshape(split), "dp", 0, 0, axis_index_groups=ORDER)
    home = lax.all_to_all(orthogonal_updates(owned), "dp", 0, 0, axis_index_groups=ORDER)
    return home.reshape(unit_count, shard_rows, width), kept


def solution(mesh):
    in_specs = (P("expert", "dp", None), P("expert", "dp", None))
    out_specs = (P("expert", "dp", None), P("expert", "dp", None))
    return jax.shard_map(shards, mesh=mesh, in_specs=in_specs, out_specs=out_specs, check_vma=False)
```

```python
import math

import jax
import jax.numpy as jnp
from jax import lax
from jax.experimental import pallas as pl
from jax.experimental.pallas import tpu as pltpu
from jax.sharding import PartitionSpec as P

ITERS = 2

MU = 0.95
COEF_A = 3.4445
COEF_B = -4.775
COEF_C = 2.0315
CLIP_RMS = 0.25
TILE = 256
SMALL = pltpu.CompilerParams(vmem_limit_bytes=16 * 1024 * 1024)
LARGE = pltpu.CompilerParams(vmem_limit_bytes=28 * 1024 * 1024)
VMEM = pl.BlockSpec(memory_space=pltpu.VMEM)
HBM = pl.BlockSpec(memory_space=pltpu.HBM)
CHUNKS = 4
ORDER = [[y * 8 + z * 2 + core for y in range(4) for core in range(2) for z in range(4)]]
AXES = ("dp", "expert")


def device(x, y, z, core):
    return (y * 8 + z // 2 * 2 + core) * 8 + z % 2 * 4 + x


COLUMNS = [
    [device(x, y, z, core) for z in range(8) for core in range(2)]
    for x in range(4) for y in range(4)
]
PLANES = [
    [device(x, y, z, core) for y in range(4) for x in range(4)]
    for z in range(8) for core in range(2)
]


def square_kernel(g_ref, o_ref, same_ref):
    count, rows, width = g_ref.shape

    def add(i, total):
        values = g_ref[pl.ds(i * 2, 2)].astype(jnp.float32)
        return total + jnp.sum((values * values).reshape(-1, 8, width), axis=0)

    total = lax.fori_loop(0, count // 2, add, jnp.zeros((8, width), jnp.float32), unroll=4)
    o_ref[...] = jnp.full(o_ref.shape, jnp.sum(total), jnp.float32)


def copies_of_squares(gradients, copies):
    return pl.pallas_call(
        square_kernel,
        in_specs=[VMEM],
        out_specs=[VMEM, VMEM],
        out_shape=[
            jax.ShapeDtypeStruct((copies, 1, 128), jnp.float32),
            jax.ShapeDtypeStruct(gradients.shape, gradients.dtype),
        ],
        input_output_aliases={0: 1},
        compiler_params=SMALL,
    )(gradients)


def sum_kernel(i_ref, o_ref):
    o_ref[...] = jnp.broadcast_to(jnp.sum(i_ref[...], axis=0, keepdims=True), o_ref.shape)


def copies_of_sum(parts, copies):
    return pl.pallas_call(
        sum_kernel,
        in_specs=[VMEM],
        out_specs=VMEM,
        out_shape=jax.ShapeDtypeStruct((copies, 1, 128), jnp.float32),
        compiler_params=SMALL,
    )(parts)


def fresh_momentum(parts, gradients, momentum, entries):
    count, rows, width = gradients.shape
    chunk = count // CHUNKS

    def kernel(p_ref, g_ref, m_ref, o_ref, k_ref, k_sems):
        def part(i):
            return pl.ds(i * chunk, chunk)

        stores = [
            pltpu.make_async_copy(o_ref.at[part(i)], k_ref.at[part(i)], k_sems.at[i])
            for i in range(CHUNKS)
        ]
        total = jnp.sum(p_ref[...], axis=0, keepdims=True)[:, :1, :1]
        factor = CLIP_RMS * math.sqrt(entries) / (jnp.sqrt(total) + 1e-06)

        def step(i, carry):
            here = pl.ds(i * 2, 2)
            buffer = MU * m_ref[here].astype(jnp.float32) + factor * g_ref[here].astype(jnp.float32)
            o_ref[here] = buffer.astype(jnp.bfloat16)
            return carry

        for i in range(CHUNKS):
            lax.fori_loop(i * chunk // 2, (i + 1) * chunk // 2, step, 0, unroll=2)
            stores[i].start()
        for store in stores:
            store.wait()

    return pl.pallas_call(
        kernel,
        in_specs=[VMEM] * 3,
        out_specs=[VMEM, HBM],
        out_shape=[jax.ShapeDtypeStruct(gradients.shape, jnp.bfloat16)] * 2,
        scratch_shapes=[
            pltpu.SemaphoreType.DMA((CHUNKS,)),
        ],
        compiler_params=SMALL,
    )(parts, gradients, momentum)


def ortho_kernel(x_ref, out_ref, ortho, gram, poly):
    for i in range(x_ref.shape[1]):
        newton_schulz(x_ref.at[:, i], out_ref.at[:, i], ortho, gram, poly)


def newton_schulz(source, out, ortho, gram, poly):
    pieces, piece, width = source.shape
    rows = pieces * piece
    step = TILE // piece
    scale = 0.2 * math.sqrt(max(rows, width))

    total = jnp.zeros((8, width), jnp.float32)
    for i in range(rows // TILE):
        values = source[i * step:(i + 1) * step].astype(jnp.float32)
        total += jnp.sum((values * values).reshape(-1, 8, width), axis=0)
    inverse = 1.0 / (jnp.sqrt(jnp.sum(total)) + 1e-07)
    for i in range(rows // TILE):
        values = source[i * step:(i + 1) * step].astype(jnp.float32).reshape(TILE, width)
        ortho[i * TILE:(i + 1) * TILE, :] = (values * inverse).astype(jnp.bfloat16)

    for iteration in range(ITERS):
        for i in range(width // TILE):
            here, right = slice(i * TILE, (i + 1) * TILE), slice(i * TILE, width)
            tiles = lax.dot_general(
                ortho[:, here], ortho[:, right], (((0,), (0,)), ((), ())),
                preferred_element_type=jnp.float32,
            ).astype(jnp.bfloat16)
            gram[here, right] = tiles
            for j in range(i + 1, width // TILE):
                gram[j * TILE:(j + 1) * TILE, here] = tiles[:, (j - i) * TILE:(j - i + 1) * TILE].T
        for i in range(width // TILE):
            here, right = slice(i * TILE, (i + 1) * TILE), slice(i * TILE, width)
            squared = jnp.dot(gram[here, :], gram[:, right], preferred_element_type=jnp.float32)
            tiles = (COEF_B * gram[here, right].astype(jnp.float32) + COEF_C * squared).astype(
                jnp.bfloat16
            )
            poly[here, right] = tiles
            for j in range(i + 1, width // TILE):
                poly[j * TILE:(j + 1) * TILE, here] = tiles[:, (j - i) * TILE:(j - i + 1) * TILE].T
        for i in range(rows // TILE):
            here = slice(i * TILE, (i + 1) * TILE)
            product = jnp.dot(ortho[here, :], poly[...], preferred_element_type=jnp.float32)
            result = (COEF_A * ortho[here, :].astype(jnp.float32) + product).astype(jnp.bfloat16)
            if iteration == ITERS - 1:
                update = (scale * result.astype(jnp.float32)).astype(jnp.bfloat16)
                out[i * step:(i + 1) * step] = update.reshape(step, piece, width)
            else:
                ortho[here, :] = result


def orthogonal_updates(matrices):
    pieces, count, piece, width = matrices.shape
    rows = pieces * piece
    return pl.pallas_call(
        ortho_kernel,
        in_specs=[VMEM],
        out_specs=VMEM,
        out_shape=jax.ShapeDtypeStruct(matrices.shape, jnp.bfloat16),
        scratch_shapes=[
            pltpu.VMEM((rows, width), jnp.bfloat16),
            pltpu.VMEM((width, width), jnp.bfloat16),
            pltpu.VMEM((width, width), jnp.bfloat16),
        ],
        compiler_params=LARGE,
        cost_estimate=pl.CostEstimate(
            flops=count * ITERS * (4 * rows * width * width + 2 * width**3),
            bytes_accessed=4 * count * rows * width,
            transcendentals=0,
        ),
    )(matrices)


def shards(gradients, momentum):
    dp_count, expert_count = lax.axis_size("dp"), lax.axis_size("expert")
    unit_count, shard_rows, width = gradients.shape
    split = (dp_count, unit_count // dp_count, shard_rows, width)
    entries = unit_count * expert_count * shard_rows * dp_count * width

    parts, gradients = copies_of_squares(gradients, len(COLUMNS[0]))
    parts = lax.all_to_all(parts, AXES, 0, 0, axis_index_groups=COLUMNS)
    parts = copies_of_sum(parts, len(PLANES[0]))
    parts = lax.all_to_all(parts, AXES, 0, 0, axis_index_groups=PLANES)
    fresh, kept = fresh_momentum(parts, gradients, momentum, entries)

    owned = lax.all_to_all(fresh.reshape(split), "dp", 0, 0, axis_index_groups=ORDER)
    home = lax.all_to_all(orthogonal_updates(owned), "dp", 0, 0, axis_index_groups=ORDER)
    return home.reshape(unit_count, shard_rows, width), kept


def solution(mesh):
    in_specs = (P("expert", "dp", None), P("expert", "dp", None))
    out_specs = (P("expert", "dp", None), P("expert", "dp", None))
    return jax.shard_map(shards, mesh=mesh, in_specs=in_specs, out_specs=out_specs, check_vma=False)
```

```python
import math

import jax
import jax.numpy as jnp
from jax import lax
from jax.experimental import pallas as pl
from jax.experimental.pallas import tpu as pltpu
from jax.sharding import PartitionSpec as P

ITERS = 2

MU = 0.95
COEF_A = 3.4445
COEF_B = -4.775
COEF_C = 2.0315
CLIP_RMS = 0.25
TILE = 256
SMALL = pltpu.CompilerParams(vmem_limit_bytes=16 * 1024 * 1024)
LARGE = pltpu.CompilerParams(vmem_limit_bytes=28 * 1024 * 1024)
VMEM = pl.BlockSpec(memory_space=pltpu.VMEM)
HBM = pl.BlockSpec(memory_space=pltpu.HBM)
ORDER = [[y * 8 + z * 2 + core for y in range(4) for core in range(2) for z in range(4)]]
AXES = ("dp", "expert")


def device(x, y, z, core):
    return (y * 8 + z // 2 * 2 + core) * 8 + z % 2 * 4 + x


COLUMNS = [
    [device(x, y, z, core) for z in range(8) for core in range(2)]
    for x in range(4) for y in range(4)
]
PLANES = [
    [device(x, y, z, core) for y in range(4) for x in range(4)]
    for z in range(8) for core in range(2)
]


def square_kernel(g_ref, o_ref, same_ref):
    count, rows, width = g_ref.shape

    def add(i, total):
        values = g_ref[pl.ds(i * 2, 2)].astype(jnp.float32)
        return total + jnp.sum((values * values).reshape(-1, 8, width), axis=0)

    total = lax.fori_loop(0, count // 2, add, jnp.zeros((8, width), jnp.float32), unroll=4)
    o_ref[...] = jnp.full(o_ref.shape, jnp.sum(total), jnp.float32)


def copies_of_squares(gradients, copies):
    return pl.pallas_call(
        square_kernel,
        in_specs=[VMEM],
        out_specs=[VMEM, VMEM],
        out_shape=[
            jax.ShapeDtypeStruct((copies, 1, 128), jnp.float32),
            jax.ShapeDtypeStruct(gradients.shape, gradients.dtype),
        ],
        input_output_aliases={0: 1},
        compiler_params=SMALL,
    )(gradients)


def sum_kernel(i_ref, o_ref):
    o_ref[...] = jnp.broadcast_to(jnp.sum(i_ref[...], axis=0, keepdims=True), o_ref.shape)


def copies_of_sum(parts, copies):
    return pl.pallas_call(
        sum_kernel,
        in_specs=[VMEM],
        out_specs=VMEM,
        out_shape=jax.ShapeDtypeStruct((copies, 1, 128), jnp.float32),
        compiler_params=SMALL,
    )(parts)


def fresh_momentum(parts, gradients, momentum, entries):
    def kernel(p_ref, g_ref, m_ref, o_ref):
        total = jnp.sum(p_ref[...], axis=0, keepdims=True)[:, :1, :1]
        factor = CLIP_RMS * math.sqrt(entries) / (jnp.sqrt(total) + 1e-06)

        def step(i, carry):
            here = pl.ds(i * 2, 2)
            buffer = MU * m_ref[here].astype(jnp.float32) + factor * g_ref[here].astype(jnp.float32)
            o_ref[here] = buffer.astype(jnp.bfloat16)
            return carry

        lax.fori_loop(0, g_ref.shape[0] // 2, step, 0, unroll=2)

    return pl.pallas_call(
        kernel,
        in_specs=[VMEM] * 3,
        out_specs=VMEM,
        out_shape=jax.ShapeDtypeStruct(gradients.shape, jnp.bfloat16),
        compiler_params=SMALL,
    )(parts, gradients, momentum)


def ortho_kernel(x_ref, f_ref, out_ref, k_ref, ortho, gram, poly, sem):
    keep = pltpu.make_async_copy(f_ref, k_ref, sem)
    keep.start()
    for i in range(x_ref.shape[1]):
        newton_schulz(x_ref.at[:, i], out_ref.at[:, i], ortho, gram, poly)
    keep.wait()


def newton_schulz(source, out, ortho, gram, poly):
    pieces, piece, width = source.shape
    rows = pieces * piece
    step = TILE // piece
    scale = 0.2 * math.sqrt(max(rows, width))

    total = jnp.zeros((8, width), jnp.float32)
    for i in range(rows // TILE):
        values = source[i * step:(i + 1) * step].astype(jnp.float32)
        total += jnp.sum((values * values).reshape(-1, 8, width), axis=0)
    inverse = 1.0 / (jnp.sqrt(jnp.sum(total)) + 1e-07)
    for i in range(rows // TILE):
        values = source[i * step:(i + 1) * step].astype(jnp.float32).reshape(TILE, width)
        ortho[i * TILE:(i + 1) * TILE, :] = (values * inverse).astype(jnp.bfloat16)

    for iteration in range(ITERS):
        for i in range(width // TILE):
            here, right = slice(i * TILE, (i + 1) * TILE), slice(i * TILE, width)
            tiles = lax.dot_general(
                ortho[:, here], ortho[:, right], (((0,), (0,)), ((), ())),
                preferred_element_type=jnp.float32,
            ).astype(jnp.bfloat16)
            gram[here, right] = tiles
            for j in range(i + 1, width // TILE):
                gram[j * TILE:(j + 1) * TILE, here] = tiles[:, (j - i) * TILE:(j - i + 1) * TILE].T
        for i in range(width // TILE):
            here, right = slice(i * TILE, (i + 1) * TILE), slice(i * TILE, width)
            squared = jnp.dot(gram[here, :], gram[:, right], preferred_element_type=jnp.float32)
            tiles = (COEF_B * gram[here, right].astype(jnp.float32) + COEF_C * squared).astype(
                jnp.bfloat16
            )
            poly[here, right] = tiles
            for j in range(i + 1, width // TILE):
                poly[j * TILE:(j + 1) * TILE, here] = tiles[:, (j - i) * TILE:(j - i + 1) * TILE].T
        for i in range(rows // TILE):
            here = slice(i * TILE, (i + 1) * TILE)
            product = jnp.dot(ortho[here, :], poly[...], preferred_element_type=jnp.float32)
            result = (COEF_A * ortho[here, :].astype(jnp.float32) + product).astype(jnp.bfloat16)
            if iteration == ITERS - 1:
                update = (scale * result.astype(jnp.float32)).astype(jnp.bfloat16)
                out[i * step:(i + 1) * step] = update.reshape(step, piece, width)
            else:
                ortho[here, :] = result


def orthogonal_updates(matrices, fresh):
    pieces, count, piece, width = matrices.shape
    rows = pieces * piece
    return pl.pallas_call(
        ortho_kernel,
        in_specs=[VMEM, VMEM],
        out_specs=[VMEM, HBM],
        out_shape=[
            jax.ShapeDtypeStruct(matrices.shape, jnp.bfloat16),
            jax.ShapeDtypeStruct(fresh.shape, jnp.bfloat16),
        ],
        scratch_shapes=[
            pltpu.VMEM((rows, width), jnp.bfloat16),
            pltpu.VMEM((width, width), jnp.bfloat16),
            pltpu.VMEM((width, width), jnp.bfloat16),
            pltpu.SemaphoreType.DMA,
        ],
        compiler_params=LARGE,
        cost_estimate=pl.CostEstimate(
            flops=count * ITERS * (4 * rows * width * width + 2 * width**3),
            bytes_accessed=4 * count * rows * width,
            transcendentals=0,
        ),
    )(matrices, fresh)


def shards(gradients, momentum):
    dp_count, expert_count = lax.axis_size("dp"), lax.axis_size("expert")
    unit_count, shard_rows, width = gradients.shape
    split = (dp_count, unit_count // dp_count, shard_rows, width)
    entries = unit_count * expert_count * shard_rows * dp_count * width

    parts, gradients = copies_of_squares(gradients, len(COLUMNS[0]))
    parts = lax.all_to_all(parts, AXES, 0, 0, axis_index_groups=COLUMNS)
    parts = copies_of_sum(parts, len(PLANES[0]))
    parts = lax.all_to_all(parts, AXES, 0, 0, axis_index_groups=PLANES)
    fresh = fresh_momentum(parts, gradients, momentum, entries)

    owned = lax.all_to_all(fresh.reshape(split), "dp", 0, 0, axis_index_groups=ORDER)
    updates, kept = orthogonal_updates(owned, fresh)
    home = lax.all_to_all(updates, "dp", 0, 0, axis_index_groups=ORDER)
    return home.reshape(unit_count, shard_rows, width), kept


def solution(mesh):
    in_specs = (P("expert", "dp", None), P("expert", "dp", None))
    out_specs = (P("expert", "dp", None), P("expert", "dp", None))
    return jax.shard_map(shards, mesh=mesh, in_specs=in_specs, out_specs=out_specs, check_vma=False)
```
